32 devices in a mesh: dp: 2 (over x), seq: 4 (over z), expert: 4 (over y, core).
Axes of the slice: x: 2, y: 2, z: 4, core: 2. Of those that a mesh axis runs over, the one named last changes fastest.
Arguments:
- tokens: bfloat16 [8192, 2048], P(('dp', 'seq', 'expert')), may hold values from -6 to 6
- grad_out: bfloat16 [8192, 2048], P(('dp', 'seq', 'expert')), may hold values from -6 to 6
- route_weights: bfloat16 [8192, 2], P(('dp', 'seq', 'expert')), may hold values from 0.099609375 to 1
- expert_ids: int32 [8192, 2], P(('dp', 'seq', 'expert')), may hold values from 0 to 63, as said below
- route_slots: int32 [8192, 2], P(('dp', 'seq', 'expert')), may hold values from 0 to 7, as said below
- w_gate: bfloat16 [64, 2048, 1024], P(('seq', 'expert')), may hold values from -0.125 to 0.125
- w_up: bfloat16 [64, 2048, 1024], P(('seq', 'expert')), may hold values from -0.125 to 0.125
- w_down: bfloat16 [64, 2048, 1024], P(('seq', 'expert')), may hold values from -0.1875 to 0.1875
Outputs:
- grad_tokens: bfloat16 [8192, 2048], P(('dp', 'seq', 'expert'))
- grad_gate: bfloat16 [64, 2048, 1024], P(('seq', 'expert'), 'dp')
- grad_up: bfloat16 [64, 2048, 1024], P(('seq', 'expert'), 'dp')
- grad_down: bfloat16 [64, 2048, 1024], P(('seq', 'expert'), 'dp')
The draws below stay inside these ranges and needn't reach their ends.
Inputs may be any that keep to these rules, and one draw needn't show every extreme that they name: `expert_ids`: in every block of 256 cells, a cell's two experts differ, each expert is named by exactly 8 of the block's routes, and the experts fall into two halves drawn from the seed with each cell naming one expert of each half. `route_slots`: within a block the routes to one expert take the slots 0 to 7, each once.
All inputs are finite; a program needn't handle non-finite values.
Results may differ from the reference program's by a relative error of at most 0.0065.
Values may be sent and summed in bfloat16 or wider, within the bound.
A program may use at most 192 MiB of HBM per device.

```python
import jax
import jax.numpy as jnp
from jax import lax

D = 2048
FF = 1024
E = 64
TOK_DEV = 256
CAP = 8
TOKENS = 8192
BLOCKS = 32
N_DP = 2


def route_draw(key):
    base = jax.random.fold_in(key, 17)
    block_total = TOKENS // TOK_DEV
    slot_count = 2 * TOK_DEV // E
    half_experts = E // 2

    def one_block(index):
        block_key = jax.random.fold_in(base, index)
        key_order, key_first, key_second, key_flip = jax.random.split(block_key, 4)
        order = jax.random.permutation(key_order, E).astype(jnp.int32)
        first = jax.random.permutation(key_first, TOK_DEV).astype(jnp.int32)
        second = jax.random.permutation(key_second, TOK_DEV).astype(jnp.int32)
        flipped = jax.random.randint(key_flip, (TOK_DEV,), 0, 2).astype(jnp.int32)
        ids_first = order[first // slot_count]
        ids_second = order[half_experts + second // slot_count]
        slot_first = first % slot_count
        slot_second = second % slot_count
        ids_pair = jnp.stack([jnp.where(flipped == 1, ids_second, ids_first), jnp.where(flipped == 1, ids_first, ids_second)], 1)
        slot_pair = jnp.stack([jnp.where(flipped == 1, slot_second, slot_first), jnp.where(flipped == 1, slot_first, slot_second)], 1)
        return (ids_pair, slot_pair)
    ids_all, slots_all = jax.vmap(one_block)(jnp.arange(block_total, dtype=jnp.int32))
    return (ids_all.reshape(TOKENS, 2).astype(jnp.int32), slots_all.reshape(TOKENS, 2).astype(jnp.int32))


def draw_expert_ids(key, part):
    return route_draw(key)[0]


def draw_route_slots(key, part):
    return route_draw(key)[1]


def steps_of(stream_key, shape, cuts, low, high):
    loudness, own = 1.0, jax.random.fold_in(stream_key, 6)
    for dim, parts in cuts:
        heights = jnp.exp(jax.random.uniform(jax.random.fold_in(own, dim), (parts,), jnp.float32, low / len(cuts), high / len(cuts)))
        loudness = loudness * jnp.repeat(heights, shape[dim] // parts).reshape([-1 if axis == dim else 1 for axis in range(len(shape))])
    return loudness


def centred(stream_key, dims, scale, most, shards=(), held_as=jnp.bfloat16):
    drawn = jax.random.normal(stream_key, dims, jnp.float32) * scale
    if len(shards) > 0:
        drawn = steps_of(stream_key, dims, shards, -0.22, 0.18) * drawn
    return jnp.clip(drawn, min=-most, max=most).astype(held_as)


def setup_inputs(seed: int = 0) -> dict:
    key_list = jax.random.split(jax.random.key(seed), 9)
    tokens = centred(key_list[0], (TOKENS, D), 1.0, 6.0, ((0, 32),))
    grad_out = centred(key_list[1], (TOKENS, D), 1.0, 6.0, ((0, 32),))
    route_weights = jnp.clip(0.099609375 + 0.9003906 * jax.random.uniform(key_list[2], (TOKENS, 2), jnp.float32) ** steps_of(key_list[2], (TOKENS, 2), ((0, 32),), -0.2, 0.2), 0.099609375, 1.0).astype(jnp.bfloat16)
    expert_ids = draw_expert_ids(jax.random.fold_in(key_list[8], 71), 0)
    route_slots = draw_route_slots(jax.random.fold_in(key_list[8], 71), 0)
    w_gate = centred(key_list[5], (E, D, FF), D ** -0.5, 0.125, ((0, 16),))
    w_up = centred(key_list[6], (E, D, FF), D ** -0.5, 0.125, ((0, 16),))
    w_down = centred(key_list[7], (E, D, FF), FF ** -0.5, 0.1875, ((0, 16),))
    return dict(tokens=tokens, grad_out=grad_out, route_weights=route_weights, expert_ids=expert_ids, route_slots=route_slots, w_gate=w_gate, w_up=w_up, w_down=w_down)


def reference(tokens, grad_out, route_weights, expert_ids, route_slots, w_gate, w_up, w_down):
    cells = jnp.arange(TOKENS, dtype=jnp.int32)
    block_of = cells // TOK_DEV
    position = (expert_ids * CAP + route_slots).astype(jnp.int32)
    table = jnp.zeros((BLOCKS, E * CAP), jnp.int32).at[block_of[:, None], position].set(
        jnp.broadcast_to(cells[:, None], (TOKENS, 2)))
    weight_table = jnp.zeros((BLOCKS, E * CAP), jnp.bfloat16).at[block_of[:, None], position].set(route_weights)
    table = table.reshape(BLOCKS, E, CAP).transpose(1, 0, 2).reshape(E, BLOCKS * CAP)
    weight_table = weight_table.reshape(BLOCKS, E, CAP).transpose(1, 0, 2).reshape(E, BLOCKS * CAP)

    def expert_work(args):
        gate_w, up_w, down_w, rows, weights = args
        rows_x = tokens[rows]
        rows_g = grad_out[rows]
        gate_pre = jnp.dot(rows_x, gate_w, preferred_element_type=jnp.float32)
        up_pre = jnp.dot(rows_x, up_w, preferred_element_type=jnp.float32)
        gate_sig = jax.nn.sigmoid(gate_pre)
        silu_g = gate_pre * gate_sig
        act = (silu_g * up_pre).astype(jnp.bfloat16)
        route_grad = (weights.astype(jnp.float32)[:, None] * rows_g.astype(jnp.float32)).astype(jnp.bfloat16)
        act_grad = jnp.dot(route_grad, down_w, preferred_element_type=jnp.float32)
        gate_grad = (act_grad * up_pre * gate_sig * (1.0 + gate_pre * (1.0 - gate_sig))).astype(jnp.bfloat16)
        up_grad = (act_grad * silu_g).astype(jnp.bfloat16)
        per_seq = rows.shape[0] // N_DP

        def split_sum(left, right):
            total = jnp.zeros((D, FF), jnp.float32)
            for seq_index in range(N_DP):
                lo = seq_index * per_seq
                part_sum = jnp.dot(left[lo:lo + per_seq].T, right[lo:lo + per_seq], preferred_element_type=jnp.float32)
                total = total + lax.optimization_barrier(part_sum.astype(jnp.bfloat16)).astype(jnp.float32)
            return total.astype(jnp.bfloat16)

        grad_g = split_sum(rows_x, gate_grad)
        grad_u = split_sum(rows_x, up_grad)
        grad_d = split_sum(route_grad, act)
        back = jnp.dot(gate_grad, gate_w.T, preferred_element_type=jnp.float32)
        back = back + jnp.dot(up_grad, up_w.T, preferred_element_type=jnp.float32)
        return grad_g, grad_u, grad_d, back.astype(jnp.bfloat16)

    grad_gate, grad_up, grad_down, route_back = lax.map(expert_work, (w_gate, w_up, w_down, table, weight_table))
    grad_tokens = jnp.zeros((TOKENS, D), jnp.float32).at[table.reshape(-1)].add(
        route_back.reshape(-1, D).astype(jnp.float32))
    return grad_tokens.astype(jnp.bfloat16), grad_gate, grad_up, grad_down
```

```python
import jax
import jax.numpy as jnp
from jax import lax
from jax.sharding import PartitionSpec as P

E = 64
BF = jnp.bfloat16
F32 = jnp.float32


def per_device(tokens, grad_out, route_weights, expert_ids, route_slots, w_gate, w_up, w_down):
    group = lax.axis_size("seq") * lax.axis_size("expert")
    el, width, ff = w_gate.shape
    cells = tokens.shape[0]
    slots = 2 * cells // E
    half = width // 2
    rows = group * slots
    dp = lax.axis_index("dp")
    position = expert_ids * slots + route_slots
    place = jnp.arange(E * slots, dtype=jnp.int32)[:, None]
    hit0 = (position[:, 0][None, :] == place).astype(BF)
    hit1 = (position[:, 1][None, :] == place).astype(BF)
    pick = hit0 + hit1
    weigh = hit0 * route_weights[:, 0][None, :] + hit1 * route_weights[:, 1][None, :]
    send_x = jnp.dot(pick, tokens, preferred_element_type=F32).astype(BF)
    send_g = jnp.dot(weigh, grad_out, preferred_element_type=F32).astype(BF)
    send_x = send_x.reshape(group, el, slots, width)
    send_g = send_g.reshape(group, el, slots, width)
    axes = ("seq", "expert")
    x = lax.all_to_all(send_x, axes, split_axis=0, concat_axis=0, tiled=True)
    g = lax.all_to_all(send_g, axes, split_axis=0, concat_axis=0, tiled=True)
    x = x.transpose(1, 0, 2, 3).reshape(el, rows, width)
    g = g.transpose(1, 0, 2, 3).reshape(el, rows, width)
    swap = [(0, 1), (1, 0)]
    far_x = lax.ppermute(lax.dynamic_slice_in_dim(x, (1 - dp) * half, half, 2), "dp", swap)
    far_g = lax.ppermute(lax.dynamic_slice_in_dim(g, (1 - dp) * half, half, 2), "dp", swap)
    my_x = lax.dynamic_slice_in_dim(x, dp * half, half, 2)
    my_g = lax.dynamic_slice_in_dim(g, dp * half, half, 2)
    gate_pre = jnp.einsum("erd,edf->erf", x, w_gate, preferred_element_type=F32)
    up_pre = jnp.einsum("erd,edf->erf", x, w_up, preferred_element_type=F32)
    act_grad = jnp.einsum("erd,edf->erf", g, w_down, preferred_element_type=F32)
    sig = jax.nn.sigmoid(gate_pre)
    silu = gate_pre * sig
    act = (silu * up_pre).astype(BF)
    gate_grad = (act_grad * up_pre * sig * (1.0 + gate_pre * (1.0 - sig))).astype(BF)
    up_grad = (act_grad * silu).astype(BF)
    far_a = lax.ppermute(act, "dp", swap)
    far_gg = lax.ppermute(gate_grad, "dp", swap)
    far_ug = lax.ppermute(up_grad, "dp", swap)
    back = jnp.einsum("erf,edf->erd", gate_grad, w_gate, preferred_element_type=F32)
    back = back + jnp.einsum("erf,edf->erd", up_grad, w_up, preferred_element_type=F32)
    back = back.astype(BF).reshape(el, group, slots, width).transpose(1, 0, 2, 3)
    returned = lax.all_to_all(back, axes, split_axis=0, concat_axis=0, tiled=True)
    returned = returned.reshape(E * slots, width)
    grad_tokens = jnp.einsum("pt,pd->td", pick, returned, preferred_element_type=F32).astype(BF)

    def wgrad(a0, a1, b0, b1):
        a = jnp.concatenate([a0, a1], 1)
        b = jnp.concatenate([b0, b1], 1)
        return jnp.einsum("erd,erf->edf", a, b, preferred_element_type=F32).astype(BF)

    return (
        grad_tokens,
        wgrad(my_x, far_x, gate_grad, far_gg),
        wgrad(my_x, far_x, up_grad, far_ug),
        wgrad(my_g, far_g, act, far_a),
    )


def solution(mesh):
    cell = P(("dp", "seq", "expert"), None)
    held = P(("seq", "expert"), None, None)
    grad = P(("seq", "expert"), "dp", None)
    return jax.shard_map(
        per_device,
        mesh=mesh,
        in_specs=(cell,) * 5 + (held,) * 3,
        out_specs=(cell, grad, grad, grad),
        check_vma=False,
    )
```

```python
import functools

import jax
import jax.numpy as jnp
from jax import lax
from jax.experimental import pallas as pl
from jax.experimental.pallas import tpu as pltpu
from jax.sharding import PartitionSpec as P

E = 64
BF = jnp.bfloat16
F32 = jnp.float32
MESH = pl.DeviceIdType.MESH
NT = (((1,), (1,)), ((), ()))


def expert_kernel(
    dims, pos, wts, tok, gro, wg, wu, wd,
    ret, xs, gs, acts, ggs, ugs,
    send, recv, wbuf, xg, hid, back,
    send_sem, recv_sem, w_sem, back_sem, ret_sem, near_sem, far_send, far_recv,
):
    group, nexp, el, slots, width, ff, nbuf = dims
    half = width // 2
    rows = group * slots
    tile = min(128, rows)
    per = tile // slots
    blocks = rows // tile
    fstep = min(ff, 256)
    dstep = min(width, 512)
    me_dp = lax.axis_index("dp")
    other = 1 - me_dp
    me = lax.axis_index("seq") * nexp + lax.axis_index("expert")

    def at(j):
        return {"seq": lax.div(j, nexp), "expert": lax.rem(j, nexp)}

    def weights(e, slot):
        return [
            pltpu.make_async_copy(w.at[e], wbuf.at[slot, i], w_sem.at[slot, i])
            for i, w in enumerate((wg, wu, wd))
        ]

    for e in range(nbuf):
        for c in weights(e, e):
            c.start()

    barrier = pltpu.get_barrier_semaphore()

    @pl.loop(1, group)
    def _(k):
        j = lax.rem(me + k, group)
        pl.semaphore_signal(barrier, inc=1, device_id=at(j), device_id_type=MESH)

    pl.semaphore_signal(barrier, inc=1, device_id={"dp": other}, device_id_type=MESH)
    pl.semaphore_wait(barrier, group)

    @pl.loop(0, el)
    def _(e):
        @pl.loop(0, blocks)
        def _(b):
            r = lax.broadcasted_iota(jnp.int32, (tile, pos.shape[1]), 0)
            place = ((b * per + lax.div(r, slots)) * el + e) * slots + lax.rem(r, slots)
            hit0 = pos[0:1, :] == place
            hit1 = pos[1:2, :] == place
            pick = (jnp.where(hit0, 1.0, 0.0) + jnp.where(hit1, 1.0, 0.0)).astype(BF)
            weigh = (jnp.where(hit0, wts[0:1, :], 0.0) + jnp.where(hit1, wts[1:2, :], 0.0)).astype(BF)

            @pl.loop(0, width // dstep)
            def _(d):
                cols = pl.ds(pl.multiple_of(d * dstep, dstep), dstep)
                devs = pl.ds(b * per, per)
                px = jnp.dot(pick, tok[:, cols], preferred_element_type=F32)
                send[e, devs, 0, :, cols] = px.reshape(per, slots, dstep).astype(BF)
                pg = jnp.dot(weigh, gro[:, cols], preferred_element_type=F32)
                send[e, devs, 1, :, cols] = pg.reshape(per, slots, dstep).astype(BF)

        pltpu.make_async_copy(send.at[e, me], recv.at[e, me], recv_sem.at[e]).start()

        @pl.loop(1, group)
        def _(k):
            j = lax.rem(me + k, group)
            pltpu.make_async_remote_copy(
                src_ref=send.at[e, j], dst_ref=recv.at[e, me],
                send_sem=send_sem.at[e], recv_sem=recv_sem.at[e],
                device_id=at(j), device_id_type=MESH,
            ).start()

    def swaps(e):
        near = pl.ds(pl.multiple_of(me_dp * half, 128), half)
        away = pl.ds(pl.multiple_of(other * half, 128), half)
        pairs = [
            (xg.at[e, 0, :, near], xg.at[e, 0, :, away], xs),
            (xg.at[e, 1, :, near], xg.at[e, 1, :, away], gs),
        ] + [(hid.at[e, i], hid.at[e, i], o) for i, o in enumerate((acts, ggs, ugs))]
        out = []
        for i, (own, sent, o) in enumerate(pairs):
            local = pltpu.make_async_copy(own, o.at[e, 0], near_sem.at[e, i])
            remote = pltpu.make_async_remote_copy(
                src_ref=sent, dst_ref=o.at[e, 1],
                send_sem=far_send.at[e, i], recv_sem=far_recv.at[e, i],
                device_id={"dp": other}, device_id_type=MESH,
            )
            out.append((local, remote))
        return out

    @pl.loop(0, el)
    def _(e):
        slot = lax.rem(e, nbuf)
        pltpu.make_async_copy(recv.at[e], recv.at[e], recv_sem.at[e]).wait()

        @pl.loop(0, blocks)
        def _(b):
            @pl.loop(0, width // dstep)
            def _(d):
                cols = pl.ds(pl.multiple_of(d * dstep, dstep), dstep)
                for i in range(2):
                    v = recv[e, pl.ds(b * per, per), i, :, cols].astype(F32)
                    xg[e, i, pl.ds(pl.multiple_of(b * tile, tile), tile), cols] = v.reshape(tile, dstep).astype(BF)

        pairs = swaps(e)
        for local, remote in pairs[:2]:
            local.start()
            remote.start()
        for c in weights(e, slot):
            c.wait()

        @pl.loop(0, ff // fstep)
        def _(f):
            cols = pl.ds(pl.multiple_of(f * fstep, fstep), fstep)

            @pl.loop(0, blocks)
            def _(b):
                rs = pl.ds(pl.multiple_of(b * tile, tile), tile)
                x = xg[e, 0, rs, :]
                gp = jnp.dot(x, wbuf[slot, 0, :, cols], preferred_element_type=F32)
                up = jnp.dot(x, wbuf[slot, 1, :, cols], preferred_element_type=F32)
                ag = jnp.dot(xg[e, 1, rs, :], wbuf[slot, 2, :, cols], preferred_element_type=F32)
                sig = jax.nn.sigmoid(gp)
                silu = gp * sig
                hid[e, 0, rs, cols] = (silu * up).astype(BF)
                hid[e, 1, rs, cols] = (ag * up * sig * (1.0 + gp * (1.0 - sig))).astype(BF)
                hid[e, 2, rs, cols] = (ag * silu).astype(BF)

        for local, remote in pairs[2:]:
            local.start()
            remote.start()

        @pl.loop(0, width // dstep)
        def _(d):
            cols = pl.ds(pl.multiple_of(d * dstep, dstep), dstep)

            @pl.loop(0, blocks)
            def _(b):
                rs = pl.ds(pl.multiple_of(b * tile, tile), tile)
                t = lax.dot_general(hid[e, 1, rs, :], wbuf[slot, 0, cols, :], NT, preferred_element_type=F32)
                t = t + lax.dot_general(hid[e, 2, rs, :], wbuf[slot, 1, cols, :], NT, preferred_element_type=F32)
                back[e, pl.ds(b * per, per), :, cols] = t.reshape(per, slots, dstep).astype(BF)

        pltpu.make_async_copy(back.at[e, me], ret.at[me, e], ret_sem).start()

        @pl.loop(1, group)
        def _(k):
            j = lax.rem(me + k, group)
            pltpu.make_async_remote_copy(
                src_ref=back.at[e, j], dst_ref=ret.at[me, e],
                send_sem=back_sem.at[e], recv_sem=ret_sem,
                device_id=at(j), device_id_type=MESH,
            ).start()

        @pl.when(e + nbuf < el)
        def _():
            for c in weights(e + nbuf, slot):
                c.start()

    @pl.loop(0, el)
    def _(e):
        for local, remote in swaps(e):
            local.wait()
            remote.wait()
        rest = pl.ds(0, group - 1)
        pltpu.make_async_copy(send.at[e, rest], send.at[e, rest], send_sem.at[e]).wait()
        pltpu.make_async_copy(back.at[e, rest], back.at[e, rest], back_sem.at[e]).wait()

    pltpu.make_async_copy(ret, ret, ret_sem).wait()


def per_device(tokens, grad_out, route_weights, expert_ids, route_slots, w_gate, w_up, w_down):
    nexp = lax.axis_size("expert")
    group = lax.axis_size("seq") * nexp
    el, width, ff = w_gate.shape
    cells = tokens.shape[0]
    slots = 2 * cells // E
    half = width // 2
    rows = group * slots
    nbuf = min(2, el)
    position = expert_ids * slots + route_slots
    dims = (group, nexp, el, slots, width, ff, nbuf)
    vmem = pl.BlockSpec(memory_space=pltpu.VMEM)
    hbm = pl.BlockSpec(memory_space=pl.ANY)
    dma = pltpu.SemaphoreType.DMA
    ret, xs, gs, acts, ggs, ugs = pl.pallas_call(
        functools.partial(expert_kernel, dims),
        out_shape=[
            jax.ShapeDtypeStruct((group, el, slots, width), BF),
            jax.ShapeDtypeStruct((el, 2, rows, half), BF),
            jax.ShapeDtypeStruct((el, 2, rows, half), BF),
            jax.ShapeDtypeStruct((el, 2, rows, ff), BF),
            jax.ShapeDtypeStruct((el, 2, rows, ff), BF),
            jax.ShapeDtypeStruct((el, 2, rows, ff), BF),
        ],
        in_specs=[vmem] * 4 + [hbm] * 3,
        out_specs=[hbm] * 6,
        scratch_shapes=[
            pltpu.VMEM((el, group, 2, slots, width), BF),
            pltpu.VMEM((el, group, 2, slots, width), BF),
            pltpu.VMEM((nbuf, 3, width, ff), BF),
            pltpu.VMEM((el, 2, rows, width), BF),
            pltpu.VMEM((el, 3, rows, ff), BF),
            pltpu.VMEM((el, group, slots, width), BF),
            dma((el,)),
            dma((el,)),
            dma((nbuf, 3)),
            dma((el,)),
            dma,
            dma((el, 5)),
            dma((el, 5)),
            dma((el, 5)),
        ],
        compiler_params=pltpu.CompilerParams(
            collective_id=0, has_side_effects=True, vmem_limit_bytes=58 * 1024 * 1024
        ),
    )(position.T, route_weights.astype(F32).T, tokens, grad_out, w_gate, w_up, w_down)

    place = jnp.arange(E * slots, dtype=jnp.int32)[None, :]
    take = (position[:, 0:1] == place).astype(BF) + (position[:, 1:2] == place).astype(BF)
    ret = ret.reshape(E * slots, width)
    grad_tokens = jnp.dot(take, ret, preferred_element_type=F32).astype(BF)

    def wgrad(a, b):
        a = a.reshape(el, 2 * rows, half)
        b = b.reshape(el, 2 * rows, ff)
        return jnp.einsum("erd,erf->edf", a, b, preferred_element_type=F32).astype(BF)

    return grad_tokens, wgrad(xs, ggs), wgrad(xs, ugs), wgrad(gs, acts)


def solution(mesh):
    cell = P(("dp", "seq", "expert"), None)
    held = P(("seq", "expert"), None, None)
    grad = P(("seq", "expert"), "dp", None)
    return jax.shard_map(
        per_device,
        mesh=mesh,
        in_specs=(cell,) * 5 + (held,) * 3,
        out_specs=(cell, grad, grad, grad),
        check_vma=False,
    )
```

```python
import functools

import jax
import jax.numpy as jnp
from jax import lax
from jax.experimental import pallas as pl
from jax.experimental.pallas import tpu as pltpu
from jax.sharding import PartitionSpec as P

E = 64
BF = jnp.bfloat16
F32 = jnp.float32
MESH = pl.DeviceIdType.MESH
NT = (((1,), (1,)), ((), ()))


def expert_kernel(
    dims, pos, wts, tok, gro, wg, wu, wd,
    ret, xs, gs, acts, ggs, ugs,
    send, recv, far, wbuf, xg, hid, back,
    send_sem, recv_sem, w_sem, back_sem, ret_sem, keep_sem, far_send, far_recv,
):
    group, nexp, el, slots, width, ff, nbuf = dims
    half = width // 2
    rows = group * slots
    tile = min(128, rows)
    per = tile // slots
    blocks = rows // tile
    fstep = min(ff, 256)
    dstep = min(width, 512)
    me_dp = lax.axis_index("dp")
    other = 1 - me_dp
    me = lax.axis_index("seq") * nexp + lax.axis_index("expert")

    def at(j):
        return {"seq": lax.div(j, nexp), "expert": lax.rem(j, nexp)}

    def weights(e, slot):
        return [
            pltpu.make_async_copy(w.at[e], wbuf.at[slot, i], w_sem.at[slot, i])
            for i, w in enumerate((wg, wu, wd))
        ]

    for c in weights(0, 0):
        c.start()

    barrier = pltpu.get_barrier_semaphore()

    @pl.loop(1, group)
    def _(k):
        j = lax.rem(me + k, group)
        pl.semaphore_signal(barrier, inc=1, device_id=at(j), device_id_type=MESH)

    pl.semaphore_signal(barrier, inc=1, device_id={"dp": other}, device_id_type=MESH)
    pl.semaphore_wait(barrier, group)

    @pl.loop(0, el)
    def _(e):
        @pl.loop(0, blocks)
        def _(b):
            r = lax.broadcasted_iota(jnp.int32, (tile, pos.shape[1]), 0)
            place = ((b * per + lax.div(r, slots)) * el + e) * slots + lax.rem(r, slots)
            hit0 = pos[0:1, :] == place
            hit1 = pos[1:2, :] == place
            pick = (jnp.where(hit0, 1.0, 0.0) + jnp.where(hit1, 1.0, 0.0)).astype(BF)
            weigh = (jnp.where(hit0, wts[0:1, :], 0.0) + jnp.where(hit1, wts[1:2, :], 0.0)).astype(BF)

            @pl.loop(0, width // dstep)
            def _(d):
                cols = pl.ds(pl.multiple_of(d * dstep, dstep), dstep)
                devs = pl.ds(b * per, per)
                px = jnp.dot(pick, tok[:, cols], preferred_element_type=F32)
                send[e, devs, 0, :, cols] = px.reshape(per, slots, dstep).astype(BF)
                pg = jnp.dot(weigh, gro[:, cols], preferred_element_type=F32)
                send[e, devs, 1, :, cols] = pg.reshape(per, slots, dstep).astype(BF)

        pltpu.make_async_copy(send.at[e, me], recv.at[e, me], recv_sem.at[e]).start()

        @pl.loop(1, group)
        def _(k):
            j = lax.rem(me + k, group)
            pltpu.make_async_remote_copy(
                src_ref=send.at[e, j], dst_ref=recv.at[e, me],
                send_sem=send_sem.at[e], recv_sem=recv_sem.at[e],
                device_id=at(j), device_id_type=MESH,
            ).start()

    def swap(e):
        return pltpu.make_async_remote_copy(
            src_ref=recv.at[e], dst_ref=far.at[e],
            send_sem=far_send.at[e], recv_sem=far_recv.at[e],
            device_id={"dp": other}, device_id_type=MESH,
        )

    def keep(e, slot, part):
        cols = pl.ds(pl.multiple_of(me_dp * half, 128), half)
        pairs = [(xg.at[slot, part, 0, :, cols], xs), (xg.at[slot, part, 1, :, cols], gs)]
        pairs += [(hid.at[slot, part, i], o) for i, o in enumerate((acts, ggs, ugs))]
        return [
            pltpu.make_async_copy(src, o.at[e, part], keep_sem.at[slot, part, i])
            for i, (src, o) in enumerate(pairs)
        ]

    def forward(e, slot, part, got):
        @pl.when(e >= nbuf)
        def _():
            for c in keep(e - nbuf, slot, part):
                c.wait()

        @pl.loop(0, blocks)
        def _(b):
            rs = pl.ds(pl.multiple_of(b * tile, tile), tile)

            @pl.loop(0, width // dstep)
            def _(d):
                cols = pl.ds(pl.multiple_of(d * dstep, dstep), dstep)
                for i in range(2):
                    v = got[e, pl.ds(b * per, per), i, :, cols].astype(F32)
                    xg[slot, part, i, rs, cols] = v.reshape(tile, dstep).astype(BF)

        copies = keep(e, slot, part)
        for c in copies[:2]:
            c.start()
        if part == 0:
            for c in weights(e, slot):
                c.wait()

        @pl.loop(0, ff // fstep)
        def _(f):
            cols = pl.ds(pl.multiple_of(f * fstep, fstep), fstep)

            @pl.loop(0, blocks)
            def _(b):
                rs = pl.ds(pl.multiple_of(b * tile, tile), tile)
                x = xg[slot, part, 0, rs, :]
                gp = jnp.dot(x, wbuf[slot, 0, :, cols], preferred_element_type=F32)
                up = jnp.dot(x, wbuf[slot, 1, :, cols], preferred_element_type=F32)
                ag = jnp.dot(xg[slot, part, 1, rs, :], wbuf[slot, 2, :, cols], preferred_element_type=F32)
                sig = jax.nn.sigmoid(gp)
                silu = gp * sig
                hid[slot, part, 0, rs, cols] = (silu * up).astype(BF)
                hid[slot, part, 1, rs, cols] = (ag * up * sig * (1.0 + gp * (1.0 - sig))).astype(BF)
                hid[slot, part, 2, rs, cols] = (ag * silu).astype(BF)

        for c in copies[2:]:
            c.start()

    def peer_rows(e):
        swap(e).wait_recv()
        forward(e, lax.rem(e, nbuf), 1, far)

    @pl.loop(0, el)
    def _(e):
        slot = lax.rem(e, nbuf)
        pltpu.make_async_copy(recv.at[e], recv.at[e], recv_sem.at[e]).wait()
        swap(e).start()
        forward(e, slot, 0, recv)

        @pl.loop(0, width // dstep)
        def _(d):
            cols = pl.ds(pl.multiple_of(d * dstep, dstep), dstep)

            @pl.loop(0, blocks)
            def _(b):
                rs = pl.ds(pl.multiple_of(b * tile, tile), tile)
                t = lax.dot_general(hid[slot, 0, 1, rs, :], wbuf[slot, 0, cols, :], NT, preferred_element_type=F32)
                t = t + lax.dot_general(hid[slot, 0, 2, rs, :], wbuf[slot, 1, cols, :], NT, preferred_element_type=F32)
                back[e, pl.ds(b * per, per), :, cols] = t.reshape(per, slots, dstep).astype(BF)

        pltpu.make_async_copy(back.at[e, me], ret.at[me, e], ret_sem).start()

        @pl.loop(1, group)
        def _(k):
            j = lax.rem(me + k, group)
            pltpu.make_async_remote_copy(
                src_ref=back.at[e, j], dst_ref=ret.at[me, e],
                send_sem=back_sem.at[e], recv_sem=ret_sem,
                device_id=at(j), device_id_type=MESH,
            ).start()

        @pl.when(e > 0)
        def _():
            peer_rows(e - 1)

        @pl.when(e + 1 < el)
        def _():
            for c in weights(e + 1, lax.rem(e + 1, nbuf)):
                c.start()

    peer_rows(el - 1)
    for e in range(el - nbuf, el):
        for part in range(2):
            for c in keep(e, e % nbuf, part):
                c.wait()

    @pl.loop(0, el)
    def _(e):
        swap(e).wait_send()
        rest = pl.ds(0, group - 1)
        pltpu.make_async_copy(send.at[e, rest], send.at[e, rest], send_sem.at[e]).wait()
        pltpu.make_async_copy(back.at[e, rest], back.at[e, rest], back_sem.at[e]).wait()

    pltpu.make_async_copy(ret, ret, ret_sem).wait()


def grads_kernel(pos, ret, xs, gs, acts, ggs, ugs, gtok, ogate, oup, odown):
    place = lax.broadcasted_iota(jnp.int32, (pos.shape[0], ret.shape[0]), 1)
    take = jnp.where(pos[:, 0:1] == place, 1.0, 0.0) + jnp.where(pos[:, 1:2] == place, 1.0, 0.0)
    gtok[...] = jnp.dot(take.astype(BF), ret[...], preferred_element_type=F32).astype(BF)
    xt = xs[0].T
    ogate[0] = jnp.dot(xt, ggs[0], preferred_element_type=F32).astype(BF)
    oup[0] = jnp.dot(xt, ugs[0], preferred_element_type=F32).astype(BF)
    odown[0] = jnp.dot(gs[0].T, acts[0], preferred_element_type=F32).astype(BF)


def per_device(tokens, grad_out, route_weights, expert_ids, route_slots, w_gate, w_up, w_down):
    nexp = lax.axis_size("expert")
    group = lax.axis_size("seq") * nexp
    el, width, ff = w_gate.shape
    cells = tokens.shape[0]
    slots = 2 * cells // E
    half = width // 2
    rows = group * slots
    nbuf = min(2, el)
    position = expert_ids * slots + route_slots
    dims = (group, nexp, el, slots, width, ff, nbuf)
    vmem = pl.BlockSpec(memory_space=pltpu.VMEM)
    hbm = pl.BlockSpec(memory_space=pl.ANY)
    dma = pltpu.SemaphoreType.DMA
    ret, xs, gs, acts, ggs, ugs = pl.pallas_call(
        functools.partial(expert_kernel, dims),
        out_shape=[
            jax.ShapeDtypeStruct((group, el, slots, width), BF),
            jax.ShapeDtypeStruct((el, 2, rows, half), BF),
            jax.ShapeDtypeStruct((el, 2, rows, half), BF),
            jax.ShapeDtypeStruct((el, 2, rows, ff), BF),
            jax.ShapeDtypeStruct((el, 2, rows, ff), BF),
            jax.ShapeDtypeStruct((el, 2, rows, ff), BF),
        ],
        in_specs=[vmem] * 4 + [hbm] * 3,
        out_specs=[hbm] * 6,
        scratch_shapes=[
            pltpu.VMEM((el, group, 2, slots, width), BF),
            pltpu.VMEM((el, group, 2, slots, width), BF),
            pltpu.VMEM((el, group, 2, slots, width), BF),
            pltpu.VMEM((nbuf, 3, width, ff), BF),
            pltpu.VMEM((nbuf, 2, 2, rows, width), BF),
            pltpu.VMEM((nbuf, 2, 3, rows, ff), BF),
            pltpu.VMEM((el, group, slots, width), BF),
            dma((el,)),
            dma((el,)),
            dma((nbuf, 3)),
            dma((el,)),
            dma,
            dma((nbuf, 2, 5)),
            dma((el,)),
            dma((el,)),
        ],
        compiler_params=pltpu.CompilerParams(
            collective_id=0, has_side_effects=True, vmem_limit_bytes=58 * 1024 * 1024
        ),
    )(position.T, route_weights.astype(F32).T, tokens, grad_out, w_gate, w_up, w_down)

    cut = 2
    dcol = half // cut
    tcol = width // (el * cut)
    deep = 2 * rows
    flat = [v.reshape(el, deep, v.shape[-1]) for v in (xs, gs, acts, ggs, ugs)]
    grad = jax.ShapeDtypeStruct((el, half, ff), BF)
    lhs = pl.BlockSpec((1, deep, dcol), lambda e, d: (e, 0, d))
    rhs = pl.BlockSpec((1, deep, ff), lambda e, d: (e, 0, 0))
    out = pl.BlockSpec((1, dcol, ff), lambda e, d: (e, d, 0))
    return pl.pallas_call(
        grads_kernel,
        grid=(el, cut),
        out_shape=[jax.ShapeDtypeStruct((cells, width), BF), grad, grad, grad],
        in_specs=[
            pl.BlockSpec((cells, 2), lambda e, d: (0, 0)),
            pl.BlockSpec((E * slots, tcol), lambda e, d: (0, e * cut + d)),
            lhs, lhs, rhs, rhs, rhs,
        ],
        out_specs=[pl.BlockSpec((cells, tcol), lambda e, d: (0, e * cut + d)), out, out, out],
        compiler_params=pltpu.CompilerParams(vmem_limit_bytes=48 * 1024 * 1024),
    )(position, ret.reshape(E * slots, width), *flat)


def solution(mesh):
    cell = P(("dp", "seq", "expert"), None)
    held = P(("seq", "expert"), None, None)
    grad = P(("seq", "expert"), "dp", None)
    return jax.shard_map(
        per_device,
        mesh=mesh,
        in_specs=(cell,) * 5 + (held,) * 3,
        out_specs=(cell, grad, grad, grad),
        check_vma=False,
    )
```
